256 devices in a mesh: row: 16 (over x_hi, z), col: 16 (over x_lo, y, core).
Axes of the slice: x: 4 (x_hi: 2, x_lo: 2; x = x_hi * 2 + x_lo), y: 4, z: 8, core: 2. Of those that a mesh axis runs over, the one named last changes fastest.
Arguments:
- tokens: bfloat16 [1792, 16384], P('row', 'col'), may hold values from -6 to 6
- gate_weight: bfloat16 [16384, 26624], P('col', 'row'), may hold values from -0.046875 to 0.046875
- up_weight: bfloat16 [16384, 26624], P('col', 'row'), may hold values from -0.046875 to 0.046875
Outputs:
- hidden: bfloat16 [1792, 26624], P('col', 'row')
The draws below stay inside these ranges and needn't reach their ends.
All inputs are finite; a program needn't handle non-finite values.
Results may differ from the reference program's by a relative error of at most 0.0012.
Values may be sent and summed in bfloat16 or wider, within the bound.
No kernel may reach another device: no remote copies, remote signals or barrier semaphores. Data moves between devices by JAX's collectives and lax.ppermute only.
A program may use at most 128 MiB of HBM per device.

```python
import jax
import jax.numpy as jnp

D = 16384
FF_WIN = 26624
TOKENS = 1792


def with_spikes(array, rng, source, target, parts, factor):
    def block_of(position):
        return (jnp.arange(array.shape[position]) // (array.shape[position] // parts)).reshape((-1,) + (1,) * (array.ndim - 1 - position))

    first = jax.random.permutation(rng, parts)[block_of(target)]
    far = (block_of(target) + parts // 2) % parts
    return jnp.where((block_of(source) == first) | (block_of(source) == far), factor * array, array)


def steps_of(stream_key, dims, split, low, top_value):
    def one(axis_at, shards_of):
        draws = jax.random.uniform(jax.random.fold_in(jax.random.fold_in(stream_key, 6), axis_at), (shards_of,), jnp.float32, low / len(split), top_value / len(split))
        return jnp.repeat(jnp.exp(draws), dims[axis_at] // shards_of).reshape((-1,) + (1,) * (len(dims) - axis_at - 1))

    factor_of = one(*split[0])
    for cut in split[1:]:
        factor_of = factor_of * one(*cut)
    return factor_of


def noise(rng, dims, deviation, bound, shards=(), kind=jnp.bfloat16):
    drawn = deviation * jax.random.normal(rng, dims, jnp.float32)
    if shards:
        drawn = drawn * steps_of(rng, dims, shards, -0.22, 0.18)
    return jnp.clip(drawn, -bound, bound).astype(kind)


def heavy_noise(rng, shape, deviation, most, pieces, heavy, kind=jnp.bfloat16):
    values = deviation * jax.random.normal(rng, shape, jnp.float32)
    if pieces:
        values = values * steps_of(rng, shape, pieces, -0.22, 0.18)
    return jnp.clip(with_spikes(values, jax.random.fold_in(rng, 3), *heavy), -most, most).astype(kind)


def setup_inputs(seed: int = 0) -> dict:
    streams_of = jax.random.split(jax.random.key(seed), 4)
    tokens = heavy_noise(streams_of[0], (TOKENS, D), 1.0, 6.0, ((0, 16), (1, 16)), (1, 0, 16, 2.0))
    gate_weight = noise(streams_of[1], (D, FF_WIN), D ** -0.5, 0.046875, ((0, 16), (1, 16)))
    up_weight = noise(streams_of[2], (D, FF_WIN), D ** -0.5, 0.046875, ((0, 16), (1, 16)))
    return {"tokens": tokens, "gate_weight": gate_weight, "up_weight": up_weight}


def reference(tokens, gate_weight, up_weight):
    gate = jnp.dot(tokens, gate_weight, preferred_element_type=jnp.float32)
    up = jnp.dot(tokens, up_weight, preferred_element_type=jnp.float32)
    return (jax.nn.silu(gate) * up).astype(jnp.bfloat16)
```

```python
import math

import jax
import jax.numpy as jnp
from jax import lax
from jax.experimental import pallas as pl
from jax.experimental.pallas import tpu as pltpu
from jax.sharding import PartitionSpec as P

NZ, NY = 8, 4
CHUNKS = (48, 64)
CA = 1024
TILE = 256
LANES = 128
SPAN = 250.0
LN2 = math.log(2.0)


def col_perm(f):
    pairs = []
    for c in range(16):
        x, y, k = f(c // 8, (c // 2) % 4, c % 2)
        pairs.append((c, x * 8 + (y % 4) * 2 + k))
    return pairs


def row_perm(f):
    pairs = []
    for r in range(16):
        x, z = f(r // 8, r % 8)
        pairs.append((r, x * 8 + z % 8))
    return pairs


CORE = col_perm(lambda x, y, k: (x, y, 1 - k))
RING_Y = col_perm(lambda x, y, k: (x, y + 1 - 2 * k, k))
SWAP_X = col_perm(lambda x, y, k: (1 - x, y, k))
UP_Z = row_perm(lambda x, z: (x, z + 1))
DOWN_Z = row_perm(lambda x, z: (x, z - 1))
FAR_X = row_perm(lambda x, z: (1 - x, z))


def over_col(a, perm):
    return lax.ppermute(a, "col", perm)


def over_row(a, perm):
    return lax.ppermute(a, "row", perm)


def encode(x, inv):
    u = jnp.abs(x) * inv
    g = u * lax.rsqrt(jnp.maximum(u, 1e-30))
    code = jnp.exp(g * (SPAN * LN2) - (SPAN * LN2 / 2))
    return jnp.where(x < 0, -code, code).astype(jnp.bfloat16)


def decode(code, scale):
    code = code.astype(jnp.float32)
    g = jnp.maximum(jnp.log(jnp.abs(code)) * (1 / (SPAN * LN2)) + 0.5, 0.0)
    value = g * g * scale
    return jnp.where(code < 0, -value, value)


def read_scale(ref):
    rows = ref.shape[0]
    return ref[rows - 16 : rows, :].astype(jnp.float32)[0:1, :]


def write_message(ref, stash, tile_of, tiles, rows):
    top = jnp.zeros((1, LANES), jnp.float32)
    for j in range(tiles):
        value = tile_of(j)
        stash[j] = value
        top = jnp.maximum(top, jnp.max(jnp.abs(value), axis=0, keepdims=True))
    top = jnp.max(top, axis=1, keepdims=True)
    scale = jnp.maximum(top * 1.01, 1e-30).astype(jnp.bfloat16)
    inv = jnp.broadcast_to(1.0 / scale.astype(jnp.float32), (1, LANES))
    for j in range(tiles):
        ref[j * rows : (j + 1) * rows, :] = encode(stash[j], inv)
    ref[tiles * rows : tiles * rows + 16, :] = jnp.broadcast_to(
        scale.astype(jnp.float32), (16, LANES)
    ).astype(jnp.bfloat16)


def lanes(j):
    return slice(j * LANES, (j + 1) * LANES)


def whole(shape):
    zeros = (0,) * len(shape)
    return pl.BlockSpec(shape, lambda i, at: zeros)


def call(kernel, at, operands, specs, outs, out_specs=None, scratch=(), grid=(1,), flops=0):
    if out_specs is None:
        out_specs = [whole(o.shape) for o in outs]
    moved = sum(a.size * a.dtype.itemsize for a in (*operands, *outs))
    return pl.pallas_call(
        kernel,
        out_shape=outs,
        grid_spec=pltpu.PrefetchScalarGridSpec(
            num_scalar_prefetch=1,
            grid=grid,
            in_specs=specs,
            out_specs=out_specs,
            scratch_shapes=list(scratch),
        ),
        compiler_params=pltpu.CompilerParams(vmem_limit_bytes=40 * 1024 * 1024),
        cost_estimate=pl.CostEstimate(flops=flops, bytes_accessed=moved, transcendentals=0),
    )(at, *operands)


def message(rows):
    return jax.ShapeDtypeStruct((rows + 16, LANES), jnp.bfloat16)


def f32(*shape):
    return jax.ShapeDtypeStruct(shape, jnp.float32)


B1, B2, B3, Y, X, XO, K, KO, Z = range(9)


def products(at, own, other, keep, recv, rc):
    n = len(own)
    width = keep.shape[1]
    depth = keep.shape[0]
    steps_a = CA // TILE
    steps = -(-width // TILE)

    def kernel(at_ref, *refs):
        owns, others = refs[:n], refs[n : 2 * n]
        wk, wr, out_a, out_b, xo, xr = refs[2 * n :]
        j = pl.program_id(0)

        @pl.when(j == 0)
        def _():
            for srcs, dst in ((owns, xo), (others, xr)):
                for s, shift in enumerate((0, -1, -2, -3, 1, 2, 3)):
                    z = lax.rem(at_ref[Z] + (shift + NZ), NZ)
                    rows = pl.ds(pl.multiple_of(z * (2 * rc), 32), 2 * rc)
                    dst[rows, :] = srcs[s][...].reshape(2 * rc, depth)
                z = lax.rem(at_ref[Z] + 4, NZ)
                for half in range(2):
                    rows = pl.ds(pl.multiple_of(z * (2 * rc) + half * rc, 16), rc)
                    dst[rows, :] = srcs[7 + half][...]

        def product():
            part = jnp.dot(xo[...], wk[...], preferred_element_type=jnp.float32)
            part += jnp.dot(xr[...], wr[...], preferred_element_type=jnp.float32)
            return part.reshape(NZ, 2, rc, TILE)

        @pl.when(j < steps_a)
        def _():
            out_a[...] = product()

        @pl.when(j >= steps_a)
        def _():
            out_b[...] = product()

    block = (NZ, 2, rc, TILE)
    return call(
        kernel,
        at,
        (*own, *other, keep, recv),
        [whole(a.shape) for a in (*own, *other)]
        + [pl.BlockSpec((depth, TILE), lambda j, at: (0, j))] * 2,
        [f32(NZ, 2, rc, CA), f32(NZ, 2, rc, width - CA)],
        [
            pl.BlockSpec(block, lambda j, at: (0, 0, 0, jnp.minimum(j, steps_a - 1))),
            pl.BlockSpec(block, lambda j, at: (0, 0, 0, jnp.maximum(j - steps_a, 0))),
        ],
        [pltpu.VMEM((16 * rc, depth), jnp.bfloat16)] * 2,
        (steps,),
        2 * 16 * rc * 2 * depth * width,
    )


def sum_along_y(at, part, which, rc, inbound=None):
    rows, tiles = 4 * rc, CA // LANES

    def kernel(at_ref, p, *refs):
        out, stash = refs[-2:]
        if inbound is not None:
            came = refs[0]
            scale = read_scale(came)

        def tile(j):
            value = p[0, :, lanes(j)]
            if inbound is not None:
                value += decode(came[j * rows : (j + 1) * rows, :], scale)
            return value

        write_message(out, stash, tile, tiles, rows)

    operands = [part.reshape(NY, rows, CA)]
    specs = [pl.BlockSpec((1, rows, CA), lambda i, at: (at[which], 0, 0))]
    if inbound is not None:
        operands.append(inbound)
        specs.append(whole(inbound.shape))
    (out,) = call(
        kernel, at, operands, specs, [message(tiles * rows)],
        scratch=[pltpu.VMEM((tiles, rows, LANES), jnp.float32)],
    )
    return out


def turn_to_x(at, part, inbound, rc):
    tiles = CA // LANES

    def kernel(at_ref, p, came, out, kept, stash):
        scale = read_scale(came)

        def half(j, x):
            terms = []
            for parity in range(2):
                start = j * 4 * rc + parity * 2 * rc + x * rc
                rows = pl.ds(pl.multiple_of(start, 16), rc)
                terms.append(
                    p[0, parity, pl.ds(x, 1), :, lanes(j)].reshape(rc, LANES)
                    + decode(came[rows, :], scale)
                )
            return terms

        write_message(
            out, stash, lambda j: jnp.concatenate(half(j, at_ref[XO]), axis=0), tiles, 2 * rc
        )
        for j in range(tiles):
            for parity, term in enumerate(half(j, at_ref[X])):
                kept[parity, :, lanes(j)] = term

    return call(
        kernel, at, (part.reshape(NY, 2, 2, rc, CA), inbound),
        [
            pl.BlockSpec((1, 2, 2, rc, CA), lambda i, at: (at[Y], 0, 0, 0, 0)),
            whole(inbound.shape),
        ],
        [message(tiles * 2 * rc), f32(2, rc, CA)],
        scratch=[pltpu.VMEM((tiles, 2 * rc, LANES), jnp.float32)],
    )


def send_over_x(at, part, rc):
    width = part.shape[-1]
    tiles, rows = width // LANES, NZ * rc

    def kernel(at_ref, p, out, stash):
        write_message(out, stash, lambda j: p[:, 0, :, lanes(j)].reshape(rows, LANES), tiles, rows)

    (out,) = call(
        kernel, at, (part,),
        [pl.BlockSpec((NZ, 1, rc, width), lambda i, at: (0, at[XO], 0, 0))],
        [message(tiles * rows)],
        scratch=[pltpu.VMEM((tiles, rows, LANES), jnp.float32)],
    )
    return out


def sum_after_x(at, part, which, rc, over_x, inbound=None):
    width = part.shape[-1]
    tiles, rows = width // LANES, 2 * rc

    def kernel(at_ref, p, mx, *refs):
        out, stash = refs[-2:]
        scale_x = read_scale(mx)
        if inbound is not None:
            came = refs[0]
            scale = read_scale(came)

        def tile(j):
            start = j * NZ * rc + at_ref[which] * rows
            value = p[0, :, 0, :, lanes(j)].reshape(rows, LANES)
            value += decode(mx[pl.ds(pl.multiple_of(start, 16), rows), :], scale_x)
            if inbound is not None:
                value += decode(came[j * rows : (j + 1) * rows, :], scale)
            return value

        write_message(out, stash, tile, tiles, rows)

    operands = [part.reshape(NY, 2, 2, rc, width), over_x]
    specs = [
        pl.BlockSpec((1, 2, 1, rc, width), lambda i, at: (at[which], 0, at[X], 0, 0)),
        whole(over_x.shape),
    ]
    if inbound is not None:
        operands.append(inbound)
        specs.append(whole(inbound.shape))
    (out,) = call(
        kernel, at, operands, specs, [message(tiles * rows)],
        scratch=[pltpu.VMEM((tiles, rows, LANES), jnp.float32)],
    )
    return out


def last_terms(at, kept_a, over_x_a, part_b, over_x_b, along_y_b, rc):
    width_b = part_b.shape[-1]
    width = CA + width_b

    def kernel(at_ref, ka, ma, pb, mb, yb, out, kept):
        sa, sb, sy = read_scale(ma), read_scale(mb), read_scale(yb)
        for place, dst in ((KO, out), (K, kept)):
            core = at_ref[place]
            for j in range(CA // LANES):
                rows = pl.ds(pl.multiple_of(j * 2 * rc + core * rc, 16), rc)
                dst[:, lanes(j)] = ka[pl.ds(core, 1), :, lanes(j)].reshape(rc, LANES) + decode(
                    ma[rows, :], sa
                )
            for j in range(width_b // LANES):
                start = j * NZ * rc + (at_ref[Y] * 2 + core) * rc
                rows = pl.ds(pl.multiple_of(start, 16), rc)
                rows_y = pl.ds(pl.multiple_of(j * 2 * rc + core * rc, 16), rc)
                dst[:, lanes(CA // LANES + j)] = (
                    pb[0, pl.ds(core, 1), 0, :, lanes(j)].reshape(rc, LANES)
                    + decode(mb[rows, :], sb)
                    + decode(yb[rows_y, :], sy)
                )

    return call(
        kernel, at,
        (kept_a, over_x_a, part_b.reshape(NY, 2, 2, rc, width_b), over_x_b, along_y_b),
        [
            whole(kept_a.shape),
            whole(over_x_a.shape),
            pl.BlockSpec((1, 2, 1, rc, width_b), lambda i, at: (at[Y], 0, at[X], 0, 0)),
            whole(over_x_b.shape),
            whole(along_y_b.shape),
        ],
        [f32(rc, width), f32(rc, width)],
    )


def per_device(tokens, gate_weight, up_weight):
    row, col = lax.axis_index("row"), lax.axis_index("col")
    x, y, core = col // 8, (col // 2) % NY, col % 2
    far, z = row // NZ, row % NZ
    toward = 1 - 2 * core
    at = jnp.stack(
        [
            (y - toward) % NY,
            (y - 2 * toward) % NY,
            (y - 3 * toward) % NY,
            y,
            x,
            1 - x,
            core,
            1 - core,
            z,
        ]
    ).astype(jnp.int32)

    first = core == 0
    keep = jnp.where(first, gate_weight, up_weight)
    recv = over_col(jnp.where(first, up_weight, gate_weight), CORE)

    gathered = []
    start, after = 0, None
    for rc in CHUNKS:
        own = tokens[start : start + rc]
        start += rc
        if after is not None:
            own, after = lax.optimization_barrier((own, after))
        other = over_row(own, FAR_X)
        pair = jnp.where(far == 0, jnp.stack((own, other)), jnp.stack((other, own)))
        ups, downs = [pair], [pair]
        for _ in range(3):
            ups.append(over_row(ups[-1], UP_Z))
            downs.append(over_row(downs[-1], DOWN_Z))
        blocks = ups + downs[1:]
        blocks += [over_row(ups[-1][0], UP_Z), over_row(downs[-1][1], DOWN_Z)]
        after = ups[3]
        gathered.append((blocks, [over_col(b, CORE) for b in blocks]))

    hidden = []
    for rc, (own, other) in zip(CHUNKS, gathered):
        part_a, part_b = products(at, own, other, keep, recv, rc)
        over_x_b = over_col(send_over_x(at, part_b, rc), SWAP_X)
        along_a = over_col(sum_along_y(at, part_a, B1, rc), RING_Y)
        along_a = over_col(sum_along_y(at, part_a, B2, rc, along_a), RING_Y)
        along_a = over_col(sum_along_y(at, part_a, B3, rc, along_a), RING_Y)
        out_a, kept_a = turn_to_x(at, part_a, along_a, rc)
        over_x_a = over_col(out_a, SWAP_X)
        along_b = over_col(sum_after_x(at, part_b, B1, rc, over_x_b), RING_Y)
        along_b = over_col(sum_after_x(at, part_b, B2, rc, over_x_b, along_b), RING_Y)
        along_b = over_col(sum_after_x(at, part_b, B3, rc, over_x_b, along_b), RING_Y)
        out, mine = last_terms(at, kept_a, over_x_a, part_b, over_x_b, along_b, rc)
        came = over_col(out, CORE)
        gate = jnp.where(first, mine, came)
        up = jnp.where(first, came, mine)
        hidden.append((jax.nn.silu(gate) * up).astype(jnp.bfloat16))
    return jnp.concatenate(hidden, axis=0)


def solution(mesh):
    return jax.shard_map(
        per_device,
        mesh=mesh,
        in_specs=(P("row", "col"), P("col", "row"), P("col", "row")),
        out_specs=P("col", "row"),
        check_vma=False,
    )
```

```python
import math

import jax
import jax.numpy as jnp
from jax import lax
from jax.experimental import pallas as pl
from jax.experimental.pallas import tpu as pltpu
from jax.sharding import PartitionSpec as P

NZ, NY = 8, 4
WIDTH_A = 1024
HALVES_A = (4, 4)
HALVES_B = (3, 2)
TILE = 256
NEAR = ((0, 0), (0, 1), (-1, 0), (-1, 1), (1, 0), (1, 1), (-2, 0), (-2, 1), (2, 0), (2, 1))
DISTANT = ((-3, 0), (-3, 1), (3, 0), (3, 1), (4, 0), (4, 1))
LANES = 128
MIB = 1024 * 1024
SPAN = 250.0
LN2 = math.log(2.0)


def col_perm(f):
    pairs = []
    for c in range(16):
        x, y, k = f(c // 8, (c // 2) % 4, c % 2)
        pairs.append((c, x * 8 + (y % 4) * 2 + k))
    return pairs


def row_perm(f):
    pairs = []
    for r in range(16):
        x, z = f(r // 8, r % 8)
        pairs.append((r, x * 8 + z % 8))
    return pairs


CORE = col_perm(lambda x, y, k: (x, y, 1 - k))
UP_Y = col_perm(lambda x, y, k: (x, y + 1, k))
DOWN_Y = col_perm(lambda x, y, k: (x, y - 1, k))
SWAP_X = col_perm(lambda x, y, k: (1 - x, y, k))
FAR_X = row_perm(lambda x, z: (1 - x, z))
UP_Z = row_perm(lambda x, z: (x, z + 1))
DOWN_Z = row_perm(lambda x, z: (x, z - 1))


def over_col(a, perm):
    return lax.ppermute(a, "col", perm)


def over_row(a, perm):
    return lax.ppermute(a, "row", perm)


def encode(x, inv):
    u = jnp.abs(x) * inv
    g = u * lax.rsqrt(jnp.maximum(u, 1e-30))
    code = jnp.exp(g * (SPAN * LN2) - (SPAN * LN2 / 2))
    return jnp.where(x < 0, -code, code).astype(jnp.bfloat16)


def decode(code, scale):
    code = code.astype(jnp.float32)
    g = jnp.maximum(jnp.log(jnp.abs(code)) * (1 / (SPAN * LN2)) + 0.5, 0.0)
    value = g * g * scale
    return jnp.where(code < 0, -value, value)


def read_scale(ref):
    rows = ref.shape[0]
    return ref[rows - 16 : rows, :].astype(jnp.float32)[0:1, :]


def write_message(ref, stash, values):
    top = jnp.zeros((1, LANES), jnp.float32)
    spans, at_row = [], 0
    for value_of in values:
        value = value_of()
        rows = slice(at_row, at_row + value.shape[0])
        spans.append(rows)
        at_row = rows.stop
        stash[rows, :] = value
        top = jnp.maximum(top, jnp.max(jnp.abs(value), axis=0, keepdims=True))
    top = jnp.max(top, axis=1, keepdims=True)
    scale = jnp.maximum(top * 1.01, 1e-30).astype(jnp.bfloat16)
    inv = jnp.broadcast_to(1.0 / scale.astype(jnp.float32), (1, LANES))
    for rows in spans:
        ref[rows, :] = encode(stash[rows, :], inv)
    ref[at_row : at_row + 16, :] = jnp.broadcast_to(
        scale.astype(jnp.float32), (16, LANES)
    ).astype(jnp.bfloat16)


def lanes(j):
    return slice(j * LANES, (j + 1) * LANES)


def whole(shape):
    zeros = (0,) * len(shape)
    return pl.BlockSpec(shape, lambda i, at: zeros)


def call(kernel, at, operands, specs, outs, out_specs=None, scratch=(), grid=(1,), flops=0, aliases={}, vmem=16):
    if out_specs is None:
        out_specs = [whole(o.shape) for o in outs]
    moved = sum(a.size * a.dtype.itemsize for a in (*operands, *outs))
    return pl.pallas_call(
        kernel,
        out_shape=outs,
        grid_spec=pltpu.PrefetchScalarGridSpec(
            num_scalar_prefetch=1,
            grid=grid,
            in_specs=specs,
            out_specs=out_specs,
            scratch_shapes=list(scratch),
        ),
        input_output_aliases=aliases,
        compiler_params=pltpu.CompilerParams(vmem_limit_bytes=vmem * MIB),
        cost_estimate=pl.CostEstimate(flops=flops, bytes_accessed=moved, transcendentals=0),
    )(at, *operands)


def message(rows):
    return jax.ShapeDtypeStruct((rows + 16, LANES), jnp.bfloat16)


def f32(*shape):
    return jax.ShapeDtypeStruct(shape, jnp.float32)


Y, YU, YD, YF, X, XO, K, KO, Z, F, FO = range(11)


def products(at, own, other, weights, places, tiles, bases=None):
    n = len(places)
    rc, depth = own[0].shape
    width = weights[0].shape[1]
    steps = len(tiles)
    in_a = WIDTH_A // TILE
    outs = [t < in_a for t in tiles]
    shapes = [f32(NZ, 2, rc, WIDTH_A)] if any(outs) else []
    shapes += [f32(NZ, 2, rc, width - WIDTH_A)] if not all(outs) else []

    def kernel(at_ref, *refs):
        owns, others = refs[:n], refs[n : 2 * n]
        gate, gate_other, up, up_other = refs[2 * n : 2 * n + 4]
        results = refs[-5 - len(shapes) : -5]
        mine, came, stage, sems_in, sems = refs[-5:]
        step = pl.program_id(0)

        def loads():
            for i in range(n):
                rows = slice(i * rc, (i + 1) * rc)
                yield pltpu.make_async_copy(owns[i], mine.at[rows, :], sems_in.at[0, i])
                yield pltpu.make_async_copy(others[i], came.at[rows, :], sems_in.at[1, i])

        @pl.when(step == 0)
        def _():
            for copy in loads():
                copy.start()
            for copy in loads():
                copy.wait()

        def stores(j):
            t = tiles[j]
            begin = (t if t < in_a else t - in_a) * TILE
            size = min(TILE, width - t * TILE)
            dst = results[0 if t < in_a else -1]
            for i, (shift, far) in enumerate(places):
                z = lax.rem(at_ref[Z] + (shift + NZ), NZ)
                yield pltpu.make_async_copy(
                    stage.at[j % 2, i * rc : (i + 1) * rc, 0:size],
                    dst.at[z, at_ref[FO if far else F], :, begin : begin + size],
                    sems.at[j % 2, i],
                )

        def multiply(slot, w, w_other):
            stage[slot] = jnp.dot(mine[...], w[...], preferred_element_type=jnp.float32) + jnp.dot(
                came[...], w_other[...], preferred_element_type=jnp.float32
            )

        for j in range(steps):

            @pl.when(step == j)
            def _():
                if j >= 2:
                    for copy in stores(j - 2):
                        copy.wait()

        @pl.when(at_ref[K] == 0)
        def _():
            multiply(lax.rem(step, 2), gate, gate_other)

        @pl.when(at_ref[K] == 1)
        def _():
            multiply(lax.rem(step, 2), up, up_other)

        for j in range(steps):

            @pl.when(step == j)
            def _():
                for copy in stores(j):
                    copy.start()
                if j == steps - 1:
                    for done in range(max(0, j - 1), steps):
                        for copy in stores(done):
                            copy.wait()

    def columns(place):
        return pl.BlockSpec((depth, TILE), lambda j, at: (0, tiles[0] + j * at[place]))

    hbm = pl.BlockSpec(memory_space=pl.ANY)
    operands = [*own, *other, *weights]
    specs = [hbm] * (2 * n) + [columns(KO), columns(KO), columns(K), columns(K)]
    aliases = {}
    for i, base in enumerate(bases or ()):
        operands.append(base)
        specs.append(hbm)
        aliases[len(operands)] = i
    return call(
        kernel,
        at,
        operands,
        specs,
        shapes,
        [hbm] * len(shapes),
        [
            pltpu.VMEM((n * rc, depth), jnp.bfloat16),
            pltpu.VMEM((n * rc, depth), jnp.bfloat16),
            pltpu.VMEM((2, n * rc, TILE), jnp.float32),
            pltpu.SemaphoreType.DMA((2, n)),
            pltpu.SemaphoreType.DMA((2, n)),
        ],
        (steps,),
        2 * n * rc * 2 * depth * TILE * steps,
        aliases,
        60,
    )


def y_block(part, which, half=None):
    rows, width = part.shape[0] * part.shape[1] * part.shape[2] // NY, part.shape[3]
    spec = pl.BlockSpec(
        (1, rows, width if half is None else width // 2),
        lambda i, at: (at[which], 0, half or 0),
    )
    return part.reshape(NY, rows, width), spec


def x_block(part, which):
    _, _, rc, width = part.shape
    spec = pl.BlockSpec((1, 2, 1, rc, width), lambda i, at: (at[which], 0, at[X], 0, 0))
    return part.reshape(NY, 2, 2, rc, width), spec


def emit(at, kernel, pairs, rows, outs=()):
    return call(
        kernel,
        at,
        [a for a, _ in pairs],
        [spec if spec is not None else whole(a.shape) for a, spec in pairs],
        [message(rows), *outs],
        scratch=[pltpu.VMEM((rows, LANES), jnp.float32)],
    )


def first_y(at, part, way):
    near = YD if way else YU
    rows = 4 * part.shape[2]
    operands = [y_block(part, YF, way), y_block(part, near, 1 - way)]
    tiles = (HALVES_A[way], HALVES_A[1 - way])

    def kernel(at_ref, far, next_to, out, stash):
        write_message(
            out,
            stash,
            [lambda j=j, p=p: p[0, :, lanes(j)] for p, n in zip((far, next_to), tiles) for j in range(n)],
        )

    return emit(at, kernel, operands, sum(tiles) * rows)[0]


def first_x(at, part):
    _, _, rc, width = part.shape
    rows = NZ * rc

    def kernel(at_ref, p, out, stash):
        write_message(
            out,
            stash,
            [lambda j=j: p[:, 0, :, lanes(j)].reshape(rows, LANES) for j in range(width // LANES)],
        )

    spec = pl.BlockSpec((NZ, 1, rc, width), lambda i, at: (0, at[XO], 0, 0))
    return emit(at, kernel, [(part, spec)], rows * width // LANES)[0]


def x_sum(at_ref, p, over_x, scale, which, j, rc):
    rows = 2 * rc
    start = (j * NY + at_ref[which]) * rows
    return p[0, :, 0, :, lanes(j)].reshape(rows, LANES) + decode(
        over_x[pl.ds(pl.multiple_of(start, 32), rows), :], scale
    )


def tiles_b(way):
    return range(HALVES_B[0]) if way == 0 else range(HALVES_B[0], sum(HALVES_B))


def second_y(at, part_a, came_a, part_b, over_x, way):
    near = YD if way else YU
    rc = part_a.shape[2]
    rows_a, rows_b = 4 * rc, 2 * rc
    n_a = HALVES_A[way]

    def kernel(at_ref, p, came, far, next_to, mx, out, stash):
        scale, scale_x = read_scale(came), read_scale(mx)
        pieces = [
            lambda j=j: p[0, :, lanes(j)] + decode(came[j * rows_a : (j + 1) * rows_a, :], scale)
            for j in range(n_a)
        ]
        pieces += [lambda j=j: x_sum(at_ref, far, mx, scale_x, YF, j, rc) for j in tiles_b(way)]
        pieces += [lambda j=j: x_sum(at_ref, next_to, mx, scale_x, near, j, rc) for j in tiles_b(1 - way)]
        write_message(out, stash, pieces)

    operands = [
        y_block(part_a, near, way),
        (came_a, None),
        x_block(part_b, YF),
        x_block(part_b, near),
        (over_x, None),
    ]
    return emit(at, kernel, operands, n_a * rows_a + sum(HALVES_B) * rows_b)[0]


def last_x(at, part, first, second):
    rc, width = part.shape[2:]
    rows = 2 * rc
    split = HALVES_A[0]

    def kernel(at_ref, p, up1, down1, up2, down2, out, kept, stash):
        scales = [read_scale(m) for m in (up1, down1, up2, down2)]

        def piece(j, x):
            half = j >= split
            at_far = j - split if half else j
            at_next = HALVES_A[1 - half] + at_far
            two, one = ((down2, scales[3]), (up1, scales[0])) if half else (
                (up2, scales[2]), (down1, scales[1])
            )
            terms = []
            for parity in range(2):
                value = p[0, parity, pl.ds(x, 1), :, lanes(j)].reshape(rc, LANES)
                for (ref, scale), place in ((two, at_far), (one, at_next)):
                    start = place * 4 * rc + parity * 2 * rc + x * rc
                    value += decode(ref[pl.ds(pl.multiple_of(start, 16), rc), :], scale)
                terms.append(value)
            return jnp.concatenate(terms, axis=0)

        write_message(
            out, stash, [lambda j=j: piece(j, at_ref[XO]) for j in range(width // LANES)]
        )
        for j in range(width // LANES):
            kept[:, lanes(j)] = piece(j, at_ref[X])

    spec = pl.BlockSpec((1, 2, 2, rc, width), lambda i, at: (at[Y], 0, 0, 0, 0))
    operands = [(part.reshape(NY, 2, 2, rc, width), spec)]
    operands += [(m, None) for m in (*first, *second)]
    return emit(at, kernel, operands, rows * width // LANES, [f32(rows, width)])


def offset_b(way, own_half):
    return HALVES_A[way] * 4 + (0 if own_half else HALVES_B[way] * 2)


def last_y(at, part, over_x, came, way):
    near = YD if way else YU
    rc = part.shape[2]
    rows = 2 * rc

    def kernel(at_ref, p, mx, m, out, stash):
        scale_x, scale = read_scale(mx), read_scale(m)

        def piece(i, j):
            start = offset_b(way, True) * rc + i * rows
            return x_sum(at_ref, p, mx, scale_x, near, j, rc) + decode(
                m[start : start + rows, :], scale
            )

        write_message(
            out, stash, [lambda i=i, j=j: piece(i, j) for i, j in enumerate(tiles_b(way))]
        )

    operands = [x_block(part, near), (over_x, None), (came, None)]
    return emit(at, kernel, operands, HALVES_B[way] * rows)[0]


def last_terms(at, kept_a, over_x_a, part_b, over_x_b, second, third):
    rc, width_b = part_b.shape[2:]
    width_a = kept_a.shape[1]
    width = width_a + width_b

    def kernel(at_ref, ka, ma, pb, mb, up2, down2, up3, down3, out, kept):
        sa, sb = read_scale(ma), read_scale(mb)
        s_two = [read_scale(up2), read_scale(down2)]
        s_three = [read_scale(up3), read_scale(down3)]

        def rows(first, core):
            return pl.ds(pl.multiple_of((first + core) * rc, 16), rc)

        for place, dst in ((KO, out), (K, kept)):
            core = at_ref[place]
            for j in range(width_a // LANES):
                dst[:, lanes(j)] = ka[rows(0, core), lanes(j)] + decode(ma[rows(2 * j, core), :], sa)
            for way in range(2):
                for i, j in enumerate(tiles_b(way)):
                    direct = (down2, up2)[way]
                    dst[:, lanes(width_a // LANES + j)] = (
                        pb[0, pl.ds(core, 1), 0, :, lanes(j)].reshape(rc, LANES)
                        + decode(mb[rows(j * NZ + at_ref[Y] * 2, core), :], sb)
                        + decode((up3, down3)[way][rows(2 * i, core), :], s_three[way])
                        + decode(
                            direct[rows(offset_b(1 - way, False) + 2 * i, core), :], s_two[1 - way]
                        )
                    )

    pairs = [
        (kept_a, None),
        (over_x_a, None),
        x_block(part_b, Y),
        (over_x_b, None),
        *((m, None) for m in (*second, *third)),
    ]
    return call(
        kernel,
        at,
        [a for a, _ in pairs],
        [spec if spec is not None else whole(a.shape) for a, spec in pairs],
        [f32(rc, width), f32(rc, width)],
    )


def after(a, *others):
    return lax.optimization_barrier((a, *others))[0]


def per_device(tokens, gate_weight, up_weight):
    row, col = lax.axis_index("row"), lax.axis_index("col")
    x, y, core = col // 8, (col // 2) % NY, col % 2
    far, z = row // NZ, row % NZ
    at = jnp.stack(
        [y, (y + 1) % NY, (y + 3) % NY, (y + 2) % NY, x, 1 - x, core, 1 - core, z, far, 1 - far]
    ).astype(jnp.int32)
    first = core == 0

    swapped = (over_col(gate_weight, CORE), over_col(up_weight, CORE))

    block = {(0, 0): tokens, (0, 1): over_row(tokens, FAR_X)}

    def onward(distance, x_far, ways=(0, 1), behind=()):
        for way in ways:
            sign = 1 if way else -1
            source = block[sign * (distance - 1), x_far]
            if behind:
                source = after(source, *behind)
            block[sign * distance, x_far] = over_row(source, DOWN_Z if way else UP_Z)

    onward(1, 0)
    onward(1, 1)
    block[1, 0], block[-1, 0], *swapped = lax.optimization_barrier(
        (block[1, 0], block[-1, 0], *swapped)
    )
    weights = (gate_weight, swapped[0], up_weight, swapped[1])
    onward(2, 0)
    onward(2, 1)
    near = [block[p] for p in NEAR], [over_col(block[p], CORE) for p in NEAR]
    onward(3, 0)
    onward(3, 1)
    tiles_a = list(range(WIDTH_A // TILE))
    tiles_rest = list(range(WIDTH_A // TILE, -(-gate_weight.shape[1] // TILE)))
    (part_a,) = products(at, *near, weights, NEAR, tiles_a)
    onward(4, 0, (1,), (part_a,))
    block[4, 1] = over_row(after(block[-3, 1], part_a), UP_Z)
    (part_b,) = products(at, *near, weights, NEAR, tiles_rest)
    own, other = [block[p] for p in DISTANT], [over_col(block[p], CORE) for p in DISTANT]

    (part_b,) = products(at, own, other, weights, DISTANT, tiles_rest, [part_b])
    sent = first_x(at, part_b)
    over_x_b = over_col(sent, SWAP_X)
    own[0] = after(own[0], sent)
    (part_a,) = products(at, own, other, weights, DISTANT, tiles_a, [part_a])
    ways = (UP_Y, DOWN_Y)
    first_hop = [over_col(first_y(at, part_a, way), perm) for way, perm in enumerate(ways)]
    second_hop = [
        over_col(second_y(at, part_a, first_hop[way], part_b, over_x_b, way), perm)
        for way, perm in enumerate(ways)
    ]
    sent, kept = last_x(at, part_a, first_hop, second_hop)
    over_x_a = over_col(sent, SWAP_X)
    third_hop = [
        over_col(last_y(at, part_b, over_x_b, second_hop[way], way), perm)
        for way, perm in enumerate(ways)
    ]
    out, mine = last_terms(at, kept, over_x_a, part_b, over_x_b, second_hop, third_hop)
    theirs = over_col(out, CORE)
    gate = jnp.where(first, mine, theirs)
    up = jnp.where(first, theirs, mine)
    return (jax.nn.silu(gate) * up).astype(jnp.bfloat16)


def solution(mesh):
    return jax.shard_map(
        per_device,
        mesh=mesh,
        in_specs=(P("row", "col"), P("col", "row"), P("col", "row")),
        out_specs=P("col", "row"),
        check_vma=False,
    )
```

```python
import math

import jax
import jax.numpy as jnp
from jax import lax
from jax.experimental import pallas as pl
from jax.experimental.pallas import tpu as pltpu
from jax.sharding import PartitionSpec as P

NZ, NY = 8, 4
WIDTH_A = 1024
HALVES_A = (4, 4)
HALVES_B = (3, 2)
TILE = 256
PLACES = tuple((shift, far) for shift in (0, 1, -1, 2, -2, 3, -3, 4) for far in (0, 1))
LANES = 128
MIB = 1024 * 1024
SPAN = 250.0
LN2 = math.log(2.0)


def col_perm(f):
    pairs = []
    for c in range(16):
        x, y, k = f(c // 8, (c // 2) % 4, c % 2)
        pairs.append((c, x * 8 + (y % 4) * 2 + k))
    return pairs


def row_perm(f):
    pairs = []
    for r in range(16):
        x, z = f(r // 8, r % 8)
        pairs.append((r, x * 8 + z % 8))
    return pairs


CORE = col_perm(lambda x, y, k: (x, y, 1 - k))
UP_Y = col_perm(lambda x, y, k: (x, y + 1, k))
DOWN_Y = col_perm(lambda x, y, k: (x, y - 1, k))
SWAP_X = col_perm(lambda x, y, k: (1 - x, y, k))
FAR_X = row_perm(lambda x, z: (1 - x, z))
UP_Z = row_perm(lambda x, z: (x, z + 1))
DOWN_Z = row_perm(lambda x, z: (x, z - 1))


def over_col(a, perm):
    return lax.ppermute(a, "col", perm)


def over_row(a, perm):
    return lax.ppermute(a, "row", perm)


def encode(x, inv):
    u = jnp.abs(x) * inv
    g = u * lax.rsqrt(jnp.maximum(u, 1e-30))
    code = jnp.exp(g * (SPAN * LN2) - (SPAN * LN2 / 2))
    return jnp.where(x < 0, -code, code).astype(jnp.bfloat16)


def decode(code, scale):
    code = code.astype(jnp.float32)
    g = jnp.maximum(jnp.log(jnp.abs(code)) * (1 / (SPAN * LN2)) + 0.5, 0.0)
    value = g * g * scale
    return jnp.where(code < 0, -value, value)


def read_scale(ref):
    rows = ref.shape[0]
    return ref[rows - 16 : rows, :].astype(jnp.float32)[0:1, :]


def write_message(ref, stash, values):
    top = jnp.zeros((1, LANES), jnp.float32)
    spans, at_row = [], 0
    for value_of in values:
        value = value_of()
        rows = slice(at_row, at_row + value.shape[0])
        spans.append(rows)
        at_row = rows.stop
        stash[rows, :] = value
        top = jnp.maximum(top, jnp.max(jnp.abs(value), axis=0, keepdims=True))
    top = jnp.max(top, axis=1, keepdims=True)
    scale = jnp.maximum(top * 1.01, 1e-30).astype(jnp.bfloat16)
    inv = jnp.broadcast_to(1.0 / scale.astype(jnp.float32), (1, LANES))
    for rows in spans:
        ref[rows, :] = encode(stash[rows, :], inv)
    ref[at_row : at_row + 16, :] = jnp.broadcast_to(
        scale.astype(jnp.float32), (16, LANES)
    ).astype(jnp.bfloat16)


def lanes(j):
    return slice(j * LANES, (j + 1) * LANES)


def whole(shape):
    zeros = (0,) * len(shape)
    return pl.BlockSpec(shape, lambda i, at: zeros)


def call(kernel, at, operands, specs, outs, out_specs=None, scratch=(), grid=(1,), flops=0, vmem=16):
    if out_specs is None:
        out_specs = [whole(o.shape) for o in outs]
    moved = sum(math.prod(a.shape) * a.dtype.itemsize for a in (*operands, *outs))
    return pl.pallas_call(
        kernel,
        out_shape=outs,
        grid_spec=pltpu.PrefetchScalarGridSpec(
            num_scalar_prefetch=1,
            grid=grid,
            in_specs=specs,
            out_specs=out_specs,
            scratch_shapes=list(scratch),
        ),
        compiler_params=pltpu.CompilerParams(vmem_limit_bytes=vmem * MIB),
        cost_estimate=pl.CostEstimate(flops=flops, bytes_accessed=moved, transcendentals=0),
    )(at, *operands)


def message(rows):
    return jax.ShapeDtypeStruct((rows + 16, LANES), jnp.bfloat16)


def f32(*shape):
    return jax.ShapeDtypeStruct(shape, jnp.float32)


Y, YU, YD, YF, X, XO, K, KO, Z, F, FO = range(11)


def products(at, own, other, weights):
    n = len(PLACES)
    rc, depth = own[0].shape
    width = weights[0].shape[1]
    in_a = WIDTH_A // TILE

    def kernel(at_ref, *refs):
        owns, others = refs[:n], refs[n : 2 * n]
        gate, gate_other, up, up_other = refs[2 * n : 2 * n + 4]
        out_a, out_b, mine, came, sems = refs[-5:]
        step = pl.program_id(0)

        def loads():
            for i, (shift, far) in enumerate(PLACES):
                z = lax.rem(at_ref[Z] + (shift + NZ), NZ)
                begin = (z * 2 + at_ref[FO if far else F]) * rc
                rows = pl.ds(pl.multiple_of(begin, 16), rc)
                yield pltpu.make_async_copy(owns[i], mine.at[rows, :], sems.at[0, i])
                yield pltpu.make_async_copy(others[i], came.at[rows, :], sems.at[1, i])

        @pl.when(step == 0)
        def _():
            for copy in loads():
                copy.start()
            for copy in loads():
                copy.wait()

        def multiply(out, w, w_other):
            out[...] = jnp.dot(mine[...], w[...], preferred_element_type=jnp.float32) + jnp.dot(
                came[...], w_other[...], preferred_element_type=jnp.float32
            )

        for out, here in ((out_a, step < in_a), (out_b, step >= in_a)):

            @pl.when(here & (at_ref[K] == 0))
            def _():
                multiply(out, gate, gate_other)

            @pl.when(here & (at_ref[K] == 1))
            def _():
                multiply(out, up, up_other)

    def tile(place):
        return pl.BlockSpec((depth, TILE), lambda j, at: (0, j * at[place]))

    tokens = n * rc
    parts = call(
        kernel,
        at,
        [*own, *other, *weights],
        [pl.BlockSpec(memory_space=pl.ANY)] * (2 * n) + [tile(KO), tile(KO), tile(K), tile(K)],
        [
            pltpu.VMEM((tokens, WIDTH_A), jnp.float32),
            pltpu.VMEM((tokens, width - WIDTH_A), jnp.float32),
        ],
        [
            pl.BlockSpec((tokens, TILE), lambda j, at: (0, jnp.minimum(j, in_a - 1))),
            pl.BlockSpec((tokens, TILE), lambda j, at: (0, jnp.maximum(j - in_a, 0))),
        ],
        [
            pltpu.VMEM((tokens, depth), jnp.bfloat16),
            pltpu.VMEM((tokens, depth), jnp.bfloat16),
            pltpu.SemaphoreType.DMA((2, n)),
        ],
        (-(-width // TILE),),
        2 * tokens * 2 * depth * width,
        vmem=50,
    )
    return [part.reshape(NZ, 2, rc, -1) for part in parts]


def y_block(part, which, half=None):
    rows, width = part.shape[0] * part.shape[1] * part.shape[2] // NY, part.shape[3]
    spec = pl.BlockSpec(
        (1, rows, width if half is None else width // 2),
        lambda i, at: (at[which], 0, half or 0),
    )
    return part.reshape(NY, rows, width), spec


def x_block(part, which):
    _, _, rc, width = part.shape
    spec = pl.BlockSpec((1, 2, 1, rc, width), lambda i, at: (at[which], 0, at[X], 0, 0))
    return part.reshape(NY, 2, 2, rc, width), spec


def emit(at, kernel, pairs, rows, outs=()):
    return call(
        kernel,
        at,
        [a for a, _ in pairs],
        [spec if spec is not None else whole(a.shape) for a, spec in pairs],
        [message(rows), *outs],
        scratch=[pltpu.VMEM((rows, LANES), jnp.float32)],
    )


def first_y(at, part, way):
    near = YD if way else YU
    rows = 4 * part.shape[2]
    operands = [y_block(part, YF, way), y_block(part, near, 1 - way)]
    tiles = (HALVES_A[way], HALVES_A[1 - way])

    def kernel(at_ref, far, next_to, out, stash):
        write_message(
            out,
            stash,
            [lambda j=j, p=p: p[0, :, lanes(j)] for p, n in zip((far, next_to), tiles) for j in range(n)],
        )

    return emit(at, kernel, operands, sum(tiles) * rows)[0]


def first_x(at, part):
    _, _, rc, width = part.shape
    rows = NZ * rc

    def kernel(at_ref, p, out, stash):
        write_message(
            out,
            stash,
            [lambda j=j: p[:, 0, :, lanes(j)].reshape(rows, LANES) for j in range(width // LANES)],
        )

    spec = pl.BlockSpec((NZ, 1, rc, width), lambda i, at: (0, at[XO], 0, 0))
    return emit(at, kernel, [(part, spec)], rows * width // LANES)[0]


def x_sum(at_ref, p, over_x, scale, which, j, rc):
    rows = 2 * rc
    start = (j * NY + at_ref[which]) * rows
    return p[0, :, 0, :, lanes(j)].reshape(rows, LANES) + decode(
        over_x[pl.ds(pl.multiple_of(start, 32), rows), :], scale
    )


def tiles_b(way):
    return range(HALVES_B[0]) if way == 0 else range(HALVES_B[0], sum(HALVES_B))


def second_y(at, part_a, came_a, part_b, over_x, way):
    near = YD if way else YU
    rc = part_a.shape[2]
    rows_a, rows_b = 4 * rc, 2 * rc
    n_a = HALVES_A[way]

    def kernel(at_ref, p, came, far, next_to, mx, out, stash):
        scale, scale_x = read_scale(came), read_scale(mx)
        pieces = [
            lambda j=j: p[0, :, lanes(j)] + decode(came[j * rows_a : (j + 1) * rows_a, :], scale)
            for j in range(n_a)
        ]
        pieces += [lambda j=j: x_sum(at_ref, far, mx, scale_x, YF, j, rc) for j in tiles_b(way)]
        pieces += [lambda j=j: x_sum(at_ref, next_to, mx, scale_x, near, j, rc) for j in tiles_b(1 - way)]
        write_message(out, stash, pieces)

    operands = [
        y_block(part_a, near, way),
        (came_a, None),
        x_block(part_b, YF),
        x_block(part_b, near),
        (over_x, None),
    ]
    return emit(at, kernel, operands, n_a * rows_a + sum(HALVES_B) * rows_b)[0]


def last_x(at, part, first, second):
    rc, width = part.shape[2:]
    rows = 2 * rc
    split = HALVES_A[0]

    def kernel(at_ref, p, up1, down1, up2, down2, out, kept, stash):
        scales = [read_scale(m) for m in (up1, down1, up2, down2)]

        def piece(j, x):
            half = j >= split
            at_far = j - split if half else j
            at_next = HALVES_A[1 - half] + at_far
            two, one = ((down2, scales[3]), (up1, scales[0])) if half else (
                (up2, scales[2]), (down1, scales[1])
            )
            terms = []
            for parity in range(2):
                value = p[0, parity, pl.ds(x, 1), :, lanes(j)].reshape(rc, LANES)
                for (ref, scale), place in ((two, at_far), (one, at_next)):
                    start = place * 4 * rc + parity * 2 * rc + x * rc
                    value += decode(ref[pl.ds(pl.multiple_of(start, 16), rc), :], scale)
                terms.append(value)
            return jnp.concatenate(terms, axis=0)

        write_message(
            out, stash, [lambda j=j: piece(j, at_ref[XO]) for j in range(width // LANES)]
        )
        for j in range(width // LANES):
            kept[:, lanes(j)] = piece(j, at_ref[X])

    spec = pl.BlockSpec((1, 2, 2, rc, width), lambda i, at: (at[Y], 0, 0, 0, 0))
    operands = [(part.reshape(NY, 2, 2, rc, width), spec)]
    operands += [(m, None) for m in (*first, *second)]
    return emit(at, kernel, operands, rows * width // LANES, [f32(rows, width)])


def offset_b(way, own_half):
    return HALVES_A[way] * 4 + (0 if own_half else HALVES_B[way] * 2)


def last_y(at, part, over_x, came, way):
    near = YD if way else YU
    rc = part.shape[2]
    rows = 2 * rc

    def kernel(at_ref, p, mx, m, out, stash):
        scale_x, scale = read_scale(mx), read_scale(m)

        def piece(i, j):
            start = offset_b(way, True) * rc + i * rows
            return x_sum(at_ref, p, mx, scale_x, near, j, rc) + decode(
                m[start : start + rows, :], scale
            )

        write_message(
            out, stash, [lambda i=i, j=j: piece(i, j) for i, j in enumerate(tiles_b(way))]
        )

    operands = [x_block(part, near), (over_x, None), (came, None)]
    return emit(at, kernel, operands, HALVES_B[way] * rows)[0]


def last_terms(at, kept_a, over_x_a, part_b, over_x_b, second, third):
    rc, width_b = part_b.shape[2:]
    width_a = kept_a.shape[1]
    width = width_a + width_b

    def kernel(at_ref, ka, ma, pb, mb, up2, down2, up3, down3, out, kept):
        sa, sb = read_scale(ma), read_scale(mb)
        s_two = [read_scale(up2), read_scale(down2)]
        s_three = [read_scale(up3), read_scale(down3)]

        def rows(first, core):
            return pl.ds(pl.multiple_of((first + core) * rc, 16), rc)

        for place, dst in ((KO, out), (K, kept)):
            core = at_ref[place]
            for j in range(width_a // LANES):
                dst[:, lanes(j)] = ka[rows(0, core), lanes(j)] + decode(ma[rows(2 * j, core), :], sa)
            for way in range(2):
                for i, j in enumerate(tiles_b(way)):
                    direct = (down2, up2)[way]
                    dst[:, lanes(width_a // LANES + j)] = (
                        pb[0, pl.ds(core, 1), 0, :, lanes(j)].reshape(rc, LANES)
                        + decode(mb[rows(j * NZ + at_ref[Y] * 2, core), :], sb)
                        + decode((up3, down3)[way][rows(2 * i, core), :], s_three[way])
                        + decode(
                            direct[rows(offset_b(1 - way, False) + 2 * i, core), :], s_two[1 - way]
                        )
                    )

    pairs = [
        (kept_a, None),
        (over_x_a, None),
        x_block(part_b, Y),
        (over_x_b, None),
        *((m, None) for m in (*second, *third)),
    ]
    return call(
        kernel,
        at,
        [a for a, _ in pairs],
        [spec if spec is not None else whole(a.shape) for a, spec in pairs],
        [f32(rc, width), f32(rc, width)],
    )


def after(a, *others):
    return lax.optimization_barrier((a, *others))[0]


def per_device(tokens, gate_weight, up_weight):
    row, col = lax.axis_index("row"), lax.axis_index("col")
    x, y, core = col // 8, (col // 2) % NY, col % 2
    far, z = row // NZ, row % NZ
    at = jnp.stack(
        [y, (y + 1) % NY, (y + 3) % NY, (y + 2) % NY, x, 1 - x, core, 1 - core, z, far, 1 - far]
    ).astype(jnp.int32)
    first = core == 0

    swapped = (over_col(gate_weight, CORE), over_col(up_weight, CORE))

    block = {(0, 0): tokens, (0, 1): over_row(tokens, FAR_X)}

    def onward(distance, x_far, ways=(0, 1), behind=()):
        for way in ways:
            sign = 1 if way else -1
            source = block[sign * (distance - 1), x_far]
            if behind:
                source = after(source, *behind)
            block[sign * distance, x_far] = over_row(source, DOWN_Z if way else UP_Z)

    def across(*shifts):
        for shift in shifts:
            block[shift, 1] = over_row(block[shift, 0], FAR_X)

    onward(1, 0)
    block[1, 0], block[-1, 0], *swapped = lax.optimization_barrier(
        (block[1, 0], block[-1, 0], *swapped)
    )
    weights = (gate_weight, swapped[0], up_weight, swapped[1])
    across(1, -1)
    onward(2, 0)
    across(2, -2)
    onward(3, 0)
    onward(4, 0, (1,))
    onward(3, 1)
    across(4)
    own, other = [block[p] for p in PLACES], [over_col(block[p], CORE) for p in PLACES]
    part_a, part_b = products(at, own, other, weights)
    over_x_b = over_col(first_x(at, part_b), SWAP_X)
    ways = (UP_Y, DOWN_Y)
    first_hop = [over_col(first_y(at, part_a, way), perm) for way, perm in enumerate(ways)]
    second_hop = [
        over_col(second_y(at, part_a, first_hop[way], part_b, over_x_b, way), perm)
        for way, perm in enumerate(ways)
    ]
    sent, kept = last_x(at, part_a, first_hop, second_hop)
    over_x_a = over_col(sent, SWAP_X)
    third_hop = [
        over_col(last_y(at, part_b, over_x_b, second_hop[way], way), perm)
        for way, perm in enumerate(ways)
    ]
    out, mine = last_terms(at, kept, over_x_a, part_b, over_x_b, second_hop, third_hop)
    theirs = over_col(out, CORE)
    gate = jnp.where(first, mine, theirs)
    up = jnp.where(first, theirs, mine)
    return (jax.nn.silu(gate) * up).astype(jnp.bfloat16)


def solution(mesh):
    return jax.shard_map(
        per_device,
        mesh=mesh,
        in_specs=(P("row", "col"), P("col", "row"), P("col", "row")),
        out_specs=P("col", "row"),
        check_vma=False,
    )
```

```python
import math

import jax
import jax.numpy as jnp
from jax import lax
from jax.experimental import pallas as pl
from jax.experimental.pallas import tpu as pltpu
from jax.sharding import PartitionSpec as P

NZ, NY = 8, 4
WIDTH_A = 1024
HALVES_A = (4, 4)
HALVES_B = (3, 2)
TILE = 256
PLACES = tuple((shift, far) for shift in (0, 1, -1, 2, -2, 3, -3, 4) for far in (0, 1))
LANES = 128
MIB = 1024 * 1024
SPAN = 250.0
LN2 = math.log(2.0)


def col_perm(f):
    pairs = []
    for c in range(16):
        x, y, k = f(c // 8, (c // 2) % 4, c % 2)
        pairs.append((c, x * 8 + (y % 4) * 2 + k))
    return pairs


def row_perm(f):
    pairs = []
    for r in range(16):
        x, z = f(r // 8, r % 8)
        pairs.append((r, x * 8 + z % 8))
    return pairs


CORE = col_perm(lambda x, y, k: (x, y, 1 - k))
UP_Y = col_perm(lambda x, y, k: (x, y + 1, k))
DOWN_Y = col_perm(lambda x, y, k: (x, y - 1, k))
SWAP_X = col_perm(lambda x, y, k: (1 - x, y, k))
FAR_X = row_perm(lambda x, z: (1 - x, z))
UP_Z = row_perm(lambda x, z: (x, z + 1))
DOWN_Z = row_perm(lambda x, z: (x, z - 1))


def over_col(a, perm):
    return lax.ppermute(a, "col", perm)


def over_row(a, perm):
    return lax.ppermute(a, "row", perm)


def encode(x, inv):
    u = jnp.abs(x) * inv
    g = u * lax.rsqrt(jnp.maximum(u, 1e-30))
    code = jnp.exp(g * (SPAN * LN2) - (SPAN * LN2 / 2))
    return jnp.where(x < 0, -code, code).astype(jnp.bfloat16)


def decode(code, scale):
    code = code.astype(jnp.float32)
    g = jnp.maximum(jnp.log(jnp.abs(code)) * (1 / (SPAN * LN2)) + 0.5, 0.0)
    value = g * g * scale
    return jnp.where(code < 0, -value, value)


def read_scale(ref):
    rows = ref.shape[0]
    return ref[rows - 16 : rows, :].astype(jnp.float32)[0:1, :]


def write_message(ref, stash, values):
    top = jnp.zeros((1, LANES), jnp.float32)
    spans, at_row = [], 0
    for value_of in values:
        value = value_of()
        rows = slice(at_row, at_row + value.shape[0])
        spans.append(rows)
        at_row = rows.stop
        stash[rows, :] = value
        top = jnp.maximum(top, jnp.max(jnp.abs(value), axis=0, keepdims=True))
    top = jnp.max(top, axis=1, keepdims=True)
    scale = jnp.maximum(top * 1.01, 1e-30).astype(jnp.bfloat16)
    inv = jnp.broadcast_to(1.0 / scale.astype(jnp.float32), (1, LANES))
    for rows in spans:
        ref[rows, :] = encode(stash[rows, :], inv)
    ref[at_row : at_row + 16, :] = jnp.broadcast_to(
        scale.astype(jnp.float32), (16, LANES)
    ).astype(jnp.bfloat16)


def lanes(j):
    return slice(j * LANES, (j + 1) * LANES)


def whole(shape):
    zeros = (0,) * len(shape)
    return pl.BlockSpec(shape, lambda i, at: zeros)


def call(kernel, at, operands, specs, outs, out_specs=None, scratch=(), grid=(1,), flops=0, vmem=16):
    if out_specs is None:
        out_specs = [whole(o.shape) for o in outs]
    moved = sum(math.prod(a.shape) * a.dtype.itemsize for a in (*operands, *outs))
    return pl.pallas_call(
        kernel,
        out_shape=outs,
        grid_spec=pltpu.PrefetchScalarGridSpec(
            num_scalar_prefetch=1,
            grid=grid,
            in_specs=specs,
            out_specs=out_specs,
            scratch_shapes=list(scratch),
        ),
        compiler_params=pltpu.CompilerParams(vmem_limit_bytes=vmem * MIB),
        cost_estimate=pl.CostEstimate(flops=flops, bytes_accessed=moved, transcendentals=0),
    )(at, *operands)


def message(rows):
    return jax.ShapeDtypeStruct((rows + 16, LANES), jnp.bfloat16)


def f32(*shape):
    return jax.ShapeDtypeStruct(shape, jnp.float32)


Y, YU, YD, YF, X, XO, K, KO, Z, F, FO = range(11)


def products(at, own, other, weights):
    n = len(PLACES)
    rc, depth = own[0].shape
    width = weights[0].shape[1]
    in_a = WIDTH_A // TILE

    def kernel(at_ref, *refs):
        owns, others = refs[:n], refs[n : 2 * n]
        gate, gate_other, up, up_other = refs[2 * n : 2 * n + 4]
        out_a, out_b, held, sems = refs[-4:]
        step = pl.program_id(0)

        def loads():
            for i, (shift, far) in enumerate(PLACES):
                z = lax.rem(at_ref[Z] + (shift + NZ), NZ)
                begin = (z * 2 + at_ref[FO if far else F]) * rc
                rows = pl.ds(pl.multiple_of(begin, 16), rc)
                yield pltpu.make_async_copy(owns[i], held.at[rows, 0:depth], sems.at[0, i])
                yield pltpu.make_async_copy(
                    others[i], held.at[rows, depth : 2 * depth], sems.at[1, i]
                )

        @pl.when(step == 0)
        def _():
            for copy in loads():
                copy.start()
            for copy in loads():
                copy.wait()

        def multiply(out, w, w_other):
            both = jnp.concatenate((w[...], w_other[...]), axis=0)
            out[...] = jnp.dot(held[...], both, preferred_element_type=jnp.float32)

        for out, here in ((out_a, step < in_a), (out_b, step >= in_a)):

            @pl.when(here & (at_ref[K] == 0))
            def _():
                multiply(out, gate, gate_other)

            @pl.when(here & (at_ref[K] == 1))
            def _():
                multiply(out, up, up_other)

    def tile(place):
        return pl.BlockSpec((depth, TILE), lambda j, at: (0, j * at[place]))

    tokens = n * rc
    parts = call(
        kernel,
        at,
        [*own, *other, *weights],
        [pl.BlockSpec(memory_space=pl.ANY)] * (2 * n) + [tile(KO), tile(KO), tile(K), tile(K)],
        [
            pltpu.VMEM((tokens, WIDTH_A), jnp.float32),
            pltpu.VMEM((tokens, width - WIDTH_A), jnp.float32),
        ],
        [
            pl.BlockSpec((tokens, TILE), lambda j, at: (0, jnp.minimum(j, in_a - 1))),
            pl.BlockSpec((tokens, TILE), lambda j, at: (0, jnp.maximum(j - in_a, 0))),
        ],
        [
            pltpu.VMEM((tokens, 2 * depth), jnp.bfloat16),
            pltpu.SemaphoreType.DMA((2, n)),
        ],
        (-(-width // TILE),),
        2 * tokens * 2 * depth * width,
        vmem=50,
    )
    return [part.reshape(NZ, 2, rc, -1) for part in parts]


def y_block(part, which, half=None):
    rows, width = part.shape[0] * part.shape[1] * part.shape[2] // NY, part.shape[3]
    spec = pl.BlockSpec(
        (1, rows, width if half is None else width // 2),
        lambda i, at: (at[which], 0, half or 0),
    )
    return part.reshape(NY, rows, width), spec


def x_block(part, which):
    _, _, rc, width = part.shape
    spec = pl.BlockSpec((1, 2, 1, rc, width), lambda i, at: (at[which], 0, at[X], 0, 0))
    return part.reshape(NY, 2, 2, rc, width), spec


def emit(at, kernel, pairs, rows, outs=()):
    return call(
        kernel,
        at,
        [a for a, _ in pairs],
        [spec if spec is not None else whole(a.shape) for a, spec in pairs],
        [message(rows), *outs],
        scratch=[pltpu.VMEM((rows, LANES), jnp.float32)],
    )


def first_y(at, part, way):
    near = YD if way else YU
    rows = 4 * part.shape[2]
    operands = [y_block(part, YF, way), y_block(part, near, 1 - way)]
    tiles = (HALVES_A[way], HALVES_A[1 - way])

    def kernel(at_ref, far, next_to, out, stash):
        write_message(
            out,
            stash,
            [lambda j=j, p=p: p[0, :, lanes(j)] for p, n in zip((far, next_to), tiles) for j in range(n)],
        )

    return emit(at, kernel, operands, sum(tiles) * rows)[0]


def first_x(at, part):
    _, _, rc, width = part.shape
    rows = NZ * rc

    def kernel(at_ref, p, out, stash):
        write_message(
            out,
            stash,
            [lambda j=j: p[:, 0, :, lanes(j)].reshape(rows, LANES) for j in range(width // LANES)],
        )

    spec = pl.BlockSpec((NZ, 1, rc, width), lambda i, at: (0, at[XO], 0, 0))
    return emit(at, kernel, [(part, spec)], rows * width // LANES)[0]


def x_sum(at_ref, p, over_x, scale, which, j, rc):
    rows = 2 * rc
    start = (j * NY + at_ref[which]) * rows
    return p[0, :, 0, :, lanes(j)].reshape(rows, LANES) + decode(
        over_x[pl.ds(pl.multiple_of(start, 32), rows), :], scale
    )


def tiles_b(way):
    return range(HALVES_B[0]) if way == 0 else range(HALVES_B[0], sum(HALVES_B))


def second_y(at, part_a, came_a, part_b, over_x, way):
    near = YD if way else YU
    rc = part_a.shape[2]
    rows_a, rows_b = 4 * rc, 2 * rc
    n_a = HALVES_A[way]

    def kernel(at_ref, p, came, far, next_to, mx, out, stash):
        scale, scale_x = read_scale(came), read_scale(mx)
        pieces = [
            lambda j=j: p[0, :, lanes(j)] + decode(came[j * rows_a : (j + 1) * rows_a, :], scale)
            for j in range(n_a)
        ]
        pieces += [lambda j=j: x_sum(at_ref, far, mx, scale_x, YF, j, rc) for j in tiles_b(way)]
        pieces += [lambda j=j: x_sum(at_ref, next_to, mx, scale_x, near, j, rc) for j in tiles_b(1 - way)]
        write_message(out, stash, pieces)

    operands = [
        y_block(part_a, near, way),
        (came_a, None),
        x_block(part_b, YF),
        x_block(part_b, near),
        (over_x, None),
    ]
    return emit(at, kernel, operands, n_a * rows_a + sum(HALVES_B) * rows_b)[0]


def last_x(at, part, first, second):
    rc, width = part.shape[2:]
    rows = 2 * rc
    split = HALVES_A[0]

    def kernel(at_ref, p, up1, down1, up2, down2, out, kept, stash):
        scales = [read_scale(m) for m in (up1, down1, up2, down2)]

        def piece(j, x):
            half = j >= split
            at_far = j - split if half else j
            at_next = HALVES_A[1 - half] + at_far
            two, one = ((down2, scales[3]), (up1, scales[0])) if half else (
                (up2, scales[2]), (down1, scales[1])
            )
            terms = []
            for parity in range(2):
                value = p[0, parity, pl.ds(x, 1), :, lanes(j)].reshape(rc, LANES)
                for (ref, scale), place in ((two, at_far), (one, at_next)):
                    start = place * 4 * rc + parity * 2 * rc + x * rc
                    value += decode(ref[pl.ds(pl.multiple_of(start, 16), rc), :], scale)
                terms.append(value)
            return jnp.concatenate(terms, axis=0)

        write_message(
            out, stash, [lambda j=j: piece(j, at_ref[XO]) for j in range(width // LANES)]
        )
        for j in range(width // LANES):
            kept[:, lanes(j)] = piece(j, at_ref[X])

    spec = pl.BlockSpec((1, 2, 2, rc, width), lambda i, at: (at[Y], 0, 0, 0, 0))
    operands = [(part.reshape(NY, 2, 2, rc, width), spec)]
    operands += [(m, None) for m in (*first, *second)]
    return emit(at, kernel, operands, rows * width // LANES, [f32(rows, width)])


def offset_b(way, own_half):
    return HALVES_A[way] * 4 + (0 if own_half else HALVES_B[way] * 2)


def last_y(at, part, over_x, came, way):
    near = YD if way else YU
    rc = part.shape[2]
    rows = 2 * rc

    def kernel(at_ref, p, mx, m, out, stash):
        scale_x, scale = read_scale(mx), read_scale(m)

        def piece(i, j):
            start = offset_b(way, True) * rc + i * rows
            return x_sum(at_ref, p, mx, scale_x, near, j, rc) + decode(
                m[start : start + rows, :], scale
            )

        write_message(
            out, stash, [lambda i=i, j=j: piece(i, j) for i, j in enumerate(tiles_b(way))]
        )

    operands = [x_block(part, near), (over_x, None), (came, None)]
    return emit(at, kernel, operands, HALVES_B[way] * rows)[0]


def last_terms(at, kept_a, over_x_a, part_b, over_x_b, second, third):
    rc, width_b = part_b.shape[2:]
    width_a = kept_a.shape[1]
    width = width_a + width_b

    def kernel(at_ref, ka, ma, pb, mb, up2, down2, up3, down3, out, kept):
        sa, sb = read_scale(ma), read_scale(mb)
        s_two = [read_scale(up2), read_scale(down2)]
        s_three = [read_scale(up3), read_scale(down3)]

        def rows(first, core):
            return pl.ds(pl.multiple_of((first + core) * rc, 16), rc)

        for place, dst in ((KO, out), (K, kept)):
            core = at_ref[place]
            for j in range(width_a // LANES):
                dst[:, lanes(j)] = ka[rows(0, core), lanes(j)] + decode(ma[rows(2 * j, core), :], sa)
            for way in range(2):
                for i, j in enumerate(tiles_b(way)):
                    direct = (down2, up2)[way]
                    dst[:, lanes(width_a // LANES + j)] = (
                        pb[0, pl.ds(core, 1), 0, :, lanes(j)].reshape(rc, LANES)
                        + decode(mb[rows(j * NZ + at_ref[Y] * 2, core), :], sb)
                        + decode((up3, down3)[way][rows(2 * i, core), :], s_three[way])
                        + decode(
                            direct[rows(offset_b(1 - way, False) + 2 * i, core), :], s_two[1 - way]
                        )
                    )

    pairs = [
        (kept_a, None),
        (over_x_a, None),
        x_block(part_b, Y),
        (over_x_b, None),
        *((m, None) for m in (*second, *third)),
    ]
    return call(
        kernel,
        at,
        [a for a, _ in pairs],
        [spec if spec is not None else whole(a.shape) for a, spec in pairs],
        [f32(rc, width), f32(rc, width)],
    )


def after(a, *others):
    return lax.optimization_barrier((a, *others))[0]


def per_device(tokens, gate_weight, up_weight):
    row, col = lax.axis_index("row"), lax.axis_index("col")
    x, y, core = col // 8, (col // 2) % NY, col % 2
    far, z = row // NZ, row % NZ
    at = jnp.stack(
        [y, (y + 1) % NY, (y + 3) % NY, (y + 2) % NY, x, 1 - x, core, 1 - core, z, far, 1 - far]
    ).astype(jnp.int32)
    first = core == 0

    swapped = (over_col(gate_weight, CORE), over_col(up_weight, CORE))

    block = {(0, 0): tokens, (0, 1): over_row(tokens, FAR_X)}

    def onward(distance, x_far, ways=(0, 1), behind=()):
        for way in ways:
            sign = 1 if way else -1
            source = block[sign * (distance - 1), x_far]
            if behind:
                source = after(source, *behind)
            block[sign * distance, x_far] = over_row(source, DOWN_Z if way else UP_Z)

    def across(*shifts):
        for shift in shifts:
            block[shift, 1] = over_row(block[shift, 0], FAR_X)

    onward(1, 0)
    block[1, 0], block[-1, 0], *swapped = lax.optimization_barrier(
        (block[1, 0], block[-1, 0], *swapped)
    )
    weights = (gate_weight, swapped[0], up_weight, swapped[1])
    onward(2, 0)
    across(1, -1)
    onward(3, 0)
    across(2, -2)
    onward(4, 0, (1,))
    across(3, -3)
    block[4, 1] = over_row(block[3, 1], DOWN_Z)
    own, other = [block[p] for p in PLACES], [over_col(block[p], CORE) for p in PLACES]
    part_a, part_b = products(at, own, other, weights)
    over_x_b = over_col(first_x(at, part_b), SWAP_X)
    ways = (UP_Y, DOWN_Y)
    first_hop = [over_col(first_y(at, part_a, way), perm) for way, perm in enumerate(ways)]
    second_hop = [
        over_col(second_y(at, part_a, first_hop[way], part_b, over_x_b, way), perm)
        for way, perm in enumerate(ways)
    ]
    sent, kept = last_x(at, part_a, first_hop, second_hop)
    over_x_a = over_col(sent, SWAP_X)
    third_hop = [
        over_col(last_y(at, part_b, over_x_b, second_hop[way], way), perm)
        for way, perm in enumerate(ways)
    ]
    out, mine = last_terms(at, kept, over_x_a, part_b, over_x_b, second_hop, third_hop)
    theirs = over_col(out, CORE)
    gate = jnp.where(first, mine, theirs)
    up = jnp.where(first, theirs, mine)
    return (jax.nn.silu(gate) * up).astype(jnp.bfloat16)


def solution(mesh):
    return jax.shard_map(
        per_device,
        mesh=mesh,
        in_specs=(P("row", "col"), P("col", "row"), P("col", "row")),
        out_specs=P("col", "row"),
        check_vma=False,
    )
```
